128 devices in a mesh: blk: 8 (over z, y_hi), sub: 16 (over y_lo, x, core).
Axes of the slice: x: 4, y: 4 (y_hi: 2, y_lo: 2; y = y_hi * 2 + y_lo), z: 4, core: 2. Of those that a mesh axis runs over, the one named last changes fastest.
Arguments:
- features: bfloat16 [131072, 64], P(('blk', 'sub')), may hold values from -6 to 6
- inv_scale: float32 [64], replicated, may hold values from 0.2 to 0.5
- direction: bfloat16 [131072, 32], P(('blk', 'sub')), may hold values from -8 to 8
- residual: float32 [131072, 32], P(('blk', 'sub')), may hold values from -14 to 14
- noise_variance: float32 [1], replicated, may hold values from 0.5 to 2
- plan: int32 [7], replicated, may hold values from 1 to 7, as said below
Outputs:
- kernel_product: float32 [131072, 32], P(('blk', 'sub'))
- inner_products: float32 [2, 32], replicated
The draws below stay inside these ranges and needn't reach their ends.
Inputs may be any that keep to these rules, and one draw needn't show every extreme that they name: `plan`: each value of 1 to 7 exactly once.
All inputs are finite; a program needn't handle non-finite values.
Results may differ from the reference program's by a relative error of at most 0.0075.
Values may be sent and summed in bfloat16 or wider, within the bound.
No kernel may reach another device: no remote copies, remote signals or barrier semaphores. Data moves between devices by JAX's collectives and lax.ppermute only.
A program may use at most 128 MiB of HBM per device.

```python
import math
import jax
import jax.numpy as jnp
from jax import lax

FEAT = 64
COLS = 32
ROWS = 1024
ROUNDS = 2
BLOCK = 16384
TOTAL = 131072
N_BLK = 8
N_SUB = 16


def row_profile(low_end, high_end):
    place = jnp.arange(TOTAL, dtype=jnp.float32) / TOTAL
    return (low_end + (high_end - low_end) * place)[:, None]


def draw_direction(key, part):
    key = jax.random.fold_in(key, 3)
    values = jnp.clip(jax.random.normal(key, (TOTAL, COLS), jnp.float32), -4.0, 4.0)
    profile = row_profile(0.6, 1.8)
    return (values * profile).astype(jnp.bfloat16)


def draw_residual(key, part):
    key = jax.random.fold_in(key, 5)
    other_key = jax.random.fold_in(key, 6)
    values = jnp.clip(jax.random.normal(key, (TOTAL, COLS), jnp.float32), -4.0, 4.0)
    own_part = jnp.clip(jax.random.normal(other_key, (TOTAL, COLS), jnp.float32), -4.0, 4.0)
    profile = row_profile(0.6, 1.8)
    return ((values + 0.6 * own_part) * profile).astype(jnp.float32)


def draw_plan(key, part):
    key = jax.random.fold_in(key, 23)
    order = jax.random.permutation(key, N_BLK - 1) + 1
    return order.astype(jnp.int32)


def shard_levels(key, extent, shards, low, top_value):
    def one(axis_at, parts):
        steps = jax.random.uniform(jax.random.fold_in(jax.random.fold_in(key, 6), axis_at), (parts,), jnp.float32, low / len(shards), top_value / len(shards))
        return jnp.repeat(jnp.exp(steps), extent[axis_at] // parts).reshape((-1,) + (1,) * (len(extent) - axis_at - 1))

    level = one(*shards[0])
    for cut in shards[1:]:
        level = level * one(*cut)
    return level


def noise(stream_key, dims, width, reach, split=(), kind=jnp.bfloat16):
    result = width * jax.random.normal(stream_key, dims, jnp.float32)
    if split:
        result = result * shard_levels(stream_key, dims, split, -0.22, 0.18)
    return jnp.clip(result, -reach, reach).astype(kind)


def setup_inputs(seed: int = 0) -> dict:
    streams_of = jax.random.split(jax.random.key(seed), 7)
    features = noise(streams_of[0], (TOTAL, FEAT), 1.0, 6.0, ((0, 128),))
    inv_scale = jnp.clip(jnp.exp(jax.random.uniform(streams_of[1], (FEAT,), jnp.float32, math.log(0.2), math.log(0.5))), 0.2, 0.5)
    direction = draw_direction(jax.random.fold_in(streams_of[6], 71), 0)
    residual = draw_residual(jax.random.fold_in(streams_of[6], 71), 0)
    noise_variance = jnp.clip(jnp.exp(jax.random.uniform(streams_of[4], (1,), jnp.float32, math.log(0.5), math.log(2.0))), 0.5, 2.0)
    plan = draw_plan(jax.random.fold_in(streams_of[6], 71), 0)
    return dict(features=features, inv_scale=inv_scale, direction=direction, residual=residual, noise_variance=noise_variance, plan=plan)


def matern_tile(left, left_norms, right, right_norms):
    cross_term = jnp.dot(left, right.T, preferred_element_type=jnp.float32)
    dist_sq = jnp.maximum(left_norms[:, None] + right_norms[None, :] - 2.0 * cross_term, 0.0)
    spread = jnp.sqrt(5.0 * dist_sq)
    return ((1.0 + spread + spread * spread / 3.0) * jnp.exp(-spread)).astype(jnp.bfloat16)

def reference(features, inv_scale, direction, residual, noise_variance, plan):
    scaled = (features.astype(jnp.float32) * inv_scale).astype(jnp.bfloat16)
    widened = scaled.astype(jnp.float32)
    sq_norms = lax.optimization_barrier(jnp.sum(widened * widened, axis=1))

    def row_tile(tile_index):
        first_row = (tile_index * ROWS).astype(jnp.int32)
        block_index = (tile_index // N_SUB).astype(jnp.int32)
        left = lax.dynamic_slice_in_dim(scaled, first_row, ROWS, 0)
        left_norms = lax.dynamic_slice_in_dim(sq_norms, first_row, ROWS, 0)
        running = jnp.zeros((ROWS, COLS), jnp.float32)
        column_blocks = [block_index] + [jnp.bitwise_xor(block_index, plan[round_index]) for round_index in range(ROUNDS)]
        for column_block in column_blocks:
            start_col = (column_block * BLOCK).astype(jnp.int32)
            right = lax.dynamic_slice_in_dim(scaled, start_col, BLOCK, 0)
            right_norms = lax.dynamic_slice_in_dim(sq_norms, start_col, BLOCK, 0)
            dir_block = lax.dynamic_slice_in_dim(direction, start_col, BLOCK, 0)
            kernel = matern_tile(left, left_norms, right, right_norms)
            running = running + jnp.dot(kernel, dir_block, preferred_element_type=jnp.float32)
        return running
    products = lax.map(row_tile, jnp.arange(TOTAL // ROWS, dtype=jnp.int32))
    kernel_product = products.reshape(TOTAL, COLS) + noise_variance[0] * direction.astype(jnp.float32)
    first_inner = lax.optimization_barrier(jnp.sum(direction.astype(jnp.float32) * kernel_product, axis=0))
    second_inner = lax.optimization_barrier(jnp.sum(residual * kernel_product, axis=0))
    inner_products = jnp.stack([first_inner, second_inner]) / TOTAL
    return (kernel_product, inner_products)
```

```python
import functools
import math

import jax
import jax.numpy as jnp
from jax import lax
from jax.experimental import pallas as pl
from jax.experimental.pallas import tpu as pltpu
from jax.sharding import Mesh, PartitionSpec as P

ROUNDS = 2
SUB = 256
NORM_ROWS = 16
LOG2E = math.log2(math.e)
F32 = jnp.float32
BF16 = jnp.bfloat16
HUB = ("yl", "x")
ALL = ("blk", "yl", "x", "core")


def norm_rows(points, norms_first):
    wide = points.astype(F32)
    norms = 5.0 * jnp.sum(wide * wide, axis=0, keepdims=True)
    high = norms.astype(BF16).astype(F32)
    middle = (norms - high).astype(BF16).astype(F32)
    low = norms - high - middle
    row = lax.broadcasted_iota(jnp.int32, (NORM_ROWS, norms.shape[1]), 0)
    at, ones_at = (0, 3) if norms_first else (3, 0)
    rows = jnp.where((row >= ones_at) & (row < ones_at + 3), 1.0, 0.0)
    for offset, part in enumerate((high, middle, low)):
        rows = jnp.where(row == at + offset, part, rows)
    return rows


def three_matern(five_dist_sq):
    clipped = jnp.maximum(five_dist_sq, 1e-30)
    spread = clipped * lax.rsqrt(clipped)
    decay = jnp.exp2(spread * (-LOG2E)).astype(BF16)
    near = spread.astype(BF16)
    return ((near + BF16(3)) * near + BF16(3)) * decay


def tiles_kernel(feat, per, forward, back, fixed_ref, moving_ref, *refs):
    refs = list(refs)
    forward_ref = refs.pop(0) if forward else None
    back_ref = refs.pop(0) if back else None
    left_ref, right_ref = refs
    fixed_count, _, rows = fixed_ref.shape
    depth = 2 * feat + NORM_ROWS

    @pl.when(pl.program_id(0) == 0)
    def _():
        for i in range(fixed_count):
            points = fixed_ref[i, :feat, :]
            wide = points.astype(F32)
            pad = jnp.zeros((left_ref.shape[2] - depth, rows), F32)
            whole = jnp.concatenate([wide * -8.0, wide * -2.0, norm_rows(points, True), pad], axis=0)
            left_ref[i] = whole.T.astype(BF16)
        if back:
            back_ref[...] = jnp.zeros_like(back_ref)

    for p in range(per):
        points = moving_ref[p, :feat, :]
        right_ref[p, :feat, :] = points
        right_ref[p, feat : 2 * feat, :] = points
        right_ref[p, 2 * feat :, :] = norm_rows(points, False).astype(BF16)

    if forward:
        tiles = [
            (p, i, c, r)
            for p in range(per)
            for i in range(fixed_count)
            for r in range(0, rows, SUB)
            for c in range(0, rows, SUB)
        ]
    else:
        tiles = [
            (p, i, c, r)
            for p in range(per)
            for i in range(fixed_count)
            for c in range(0, rows, SUB)
            for r in range(0, rows, SUB)
        ]
    squares, values, forward_sums, back_sums = {}, {}, {}, {}

    def add(sums, key, term):
        sums[key] = sums[key] + term if key in sums else term

    for t in range(len(tiles) + 2):
        if t < len(tiles):
            p, i, c, r = tiles[t]
            squares[t] = jnp.dot(
                left_ref[i, c : c + SUB, :depth],
                right_ref[p, :, r : r + SUB],
                preferred_element_type=F32,
            )
        if 1 <= t <= len(tiles):
            values[t - 1] = three_matern(squares.pop(t - 1))
        if t >= 2:
            p, i, c, r = tiles[t - 2]
            tile = values.pop(t - 2)
            if forward:
                dirs = fixed_ref[i, feat:, c : c + SUB]
                add(forward_sums, (p, r), jnp.dot(dirs, tile, preferred_element_type=F32))
            if back:
                dirs = moving_ref[p, feat:, r : r + SUB]
                term = lax.dot_general(
                    dirs, tile, (((1,), (1,)), ((), ())), preferred_element_type=F32
                )
                add(back_sums, (i, c), term)
    for (p, r), total in forward_sums.items():
        forward_ref[p, :, r : r + SUB] = (total * (1.0 / 3.0)).astype(forward_ref.dtype)
    for (i, c), total in back_sums.items():
        back_ref[i, :, c : c + SUB] += total * (1.0 / 3.0)


def tiles_call(fixed, moving, feat, forward, back, per):
    fixed_count, height, rows = fixed.shape
    moving_count = moving.shape[0]
    cols = height - feat
    depth = 2 * feat + NORM_ROWS
    out_shape, out_specs = [], []
    if forward:
        out_shape.append(jax.ShapeDtypeStruct((moving_count, cols, rows), BF16))
        out_specs.append(pl.BlockSpec((per, cols, rows), lambda j: (j, 0, 0)))
    if back:
        out_shape.append(jax.ShapeDtypeStruct((fixed_count, cols, rows), F32))
        out_specs.append(pl.BlockSpec((fixed_count, cols, rows), lambda j: (0, 0, 0)))
    evals = fixed_count * moving_count * rows * rows
    return pl.pallas_call(
        functools.partial(tiles_kernel, feat, per, forward, back),
        grid=(moving_count // per,),
        in_specs=[
            pl.BlockSpec((fixed_count, height, rows), lambda j: (0, 0, 0)),
            pl.BlockSpec((per, height, rows), lambda j: (j, 0, 0)),
        ],
        out_specs=out_specs,
        out_shape=out_shape,
        scratch_shapes=[
            pltpu.VMEM((fixed_count, rows, 256), BF16),
            pltpu.VMEM((per, depth, rows), BF16),
        ],
        compiler_params=pltpu.CompilerParams(vmem_limit_bytes=40 * 2**20),
        cost_estimate=pl.CostEstimate(
            flops=2 * evals * 512, bytes_accessed=moving.size * 2, transcendentals=2 * evals
        ),
    )(fixed, moving)


def pair_routes(mask, blocks, cores, reverse):
    routes = []
    for block in range(blocks):
        other = block ^ mask
        for core in range(cores):
            from_core = core if block < other else core ^ 1
            source, target = other * cores + from_core, block * cores + core
            routes.append((target, source) if reverse else (source, target))
    return routes


def over_pairs(plan, arrays, reverse):
    blocks, cores = lax.axis_size("blk"), lax.axis_size("core")
    masks = [(a, b) for a in range(1, blocks) for b in range(a + 1, blocks)]
    first, second = jnp.minimum(plan[0], plan[1]), jnp.maximum(plan[0], plan[1])
    place = (first - 1) * (2 * blocks - 2 - first) // 2 + (second - first - 1)

    def branch(pair):
        def send(*values):
            return tuple(
                lax.ppermute(value, ("blk", "core"), pair_routes(mask, blocks, cores, reverse))
                for value, mask in zip(values, pair)
            )

        return send

    return lax.switch(place, [branch(pair) for pair in masks], *arrays)


def to_owners(parts):
    yl_size, x_size = lax.axis_size("yl"), lax.axis_size("x")
    yl, x = lax.axis_index("yl"), lax.axis_index("x")
    parts = parts.reshape(yl_size, x_size, *parts.shape[1:])
    mine = lax.dynamic_index_in_dim(parts, yl, 0, keepdims=False)
    other = lax.dynamic_index_in_dim(parts, 1 - yl, 0, keepdims=False)
    arrived = lax.ppermute(other, "yl", [(i, i ^ 1) for i in range(yl_size)])
    half = mine.astype(F32) + arrived.astype(F32)
    total = lax.dynamic_index_in_dim(half, x, 0, keepdims=False)
    narrow = half.astype(BF16)
    for shift in range(1, x_size):
        sent = lax.dynamic_index_in_dim(narrow, jnp.bitwise_xor(x, shift), 0, keepdims=False)
        total = total + lax.ppermute(sent, "x", [(i, i ^ shift) for i in range(x_size)])
    return total


def shards(features, inv_scale, direction, residual, noise_variance, plan):
    feat = features.shape[1]
    rows, cols = direction.shape
    scaled = (features.astype(F32) * inv_scale).astype(BF16)
    packet = jnp.concatenate([scaled.T, direction.T], axis=0)
    gathered = lax.all_gather(packet, HUB, axis=0, tiled=False)
    partners = jnp.stack(over_pairs(plan, (packet, packet), False))
    forward, back = tiles_call(partners, gathered, feat, True, True, 1)
    other_core = [(0, 1), (1, 0)]
    mates = lax.ppermute(gathered, "core", other_core)
    narrow_back = back.astype(BF16)
    back_parts = over_pairs(plan, (narrow_back[0], narrow_back[1]), True)
    own_forward = to_owners(forward)
    (own_near,) = tiles_call(packet[None], gathered, feat, False, True, 2)
    (own_far,) = tiles_call(packet[None], mates, feat, False, True, 2)
    wide_dirs = direction.T.astype(F32)
    product = own_near[0] + own_far[0] + own_forward
    for part in back_parts:
        product = product + part.astype(F32)
    product = product + noise_variance[0] * wide_dirs
    inner = jnp.stack([jnp.sum(wide_dirs * product, axis=1), jnp.sum(residual.T * product, axis=1)])
    device_count = math.prod(lax.axis_size(axis) for axis in ALL)
    copies = jnp.broadcast_to(inner.reshape(1, 2 * cols), (device_count, 2 * cols))
    partials = lax.all_to_all(copies, ALL, 0, 0, tiled=True)
    totals = jnp.sum(partials, axis=0).reshape(2, cols)
    return (product.T, totals / (rows * device_count))


def solution(mesh):
    yl_size, cores = 2, 2
    groups = mesh.shape["sub"]
    split = mesh.devices.reshape(mesh.shape["blk"], yl_size, groups // (yl_size * cores), cores)
    by_rows = P(ALL, None)
    return jax.shard_map(
        shards,
        mesh=Mesh(split, ALL),
        in_specs=(by_rows, P(), by_rows, by_rows, P(), P()),
        out_specs=(by_rows, P()),
        check_vma=False,
    )
```

```python
import functools
import math

import jax
import jax.numpy as jnp
from jax import lax
from jax.experimental import pallas as pl
from jax.experimental.pallas import tpu as pltpu
from jax.sharding import Mesh, PartitionSpec as P

ROUNDS = 2
SUB = 256
NORM_ROWS = 16
LOG2E = math.log2(math.e)
F32 = jnp.float32
BF16 = jnp.bfloat16
ALL = ("blk", "yl", "x", "core")


def norm_rows(points, norms_first):
    wide = points.astype(F32)
    norms = 5.0 * jnp.sum(wide * wide, axis=0, keepdims=True)
    high = norms.astype(BF16).astype(F32)
    middle = (norms - high).astype(BF16).astype(F32)
    low = norms - high - middle
    row = lax.broadcasted_iota(jnp.int32, (NORM_ROWS, norms.shape[1]), 0)
    at, ones_at = (0, 3) if norms_first else (3, 0)
    rows = jnp.where((row >= ones_at) & (row < ones_at + 3), 1.0, 0.0)
    for offset, part in enumerate((high, middle, low)):
        rows = jnp.where(row == at + offset, part, rows)
    return rows


def three_matern(five_dist_sq):
    clipped = jnp.maximum(five_dist_sq, 1e-30)
    spread = clipped * lax.rsqrt(clipped)
    decay = jnp.exp2(spread * (-LOG2E)).astype(BF16)
    near = spread.astype(BF16)
    return ((near + BF16(3)) * near + BF16(3)) * decay


def tiles_kernel(feat, fixed_count, moving_count, per, forward, carry, *refs):
    refs = list(refs)
    fixed_refs = [refs.pop(0) for _ in range(fixed_count)]
    moving_refs = [refs.pop(0) for _ in range(moving_count)]
    carry_ref = refs.pop(0) if carry else None
    forward_ref = refs.pop(0) if forward else None
    back_ref, left_ref, right_ref, dirs_ref = refs
    rows = right_ref.shape[2]
    depth = 2 * feat + NORM_ROWS
    step = pl.program_id(0)

    @pl.when(step == 0)
    def _():
        for i, fixed_ref in enumerate(fixed_refs):
            points = fixed_ref[:feat, :]
            wide = points.astype(F32)
            pad = jnp.zeros((left_ref.shape[2] - depth, rows), F32)
            whole = jnp.concatenate([wide * -8.0, wide * -2.0, norm_rows(points, True), pad], axis=0)
            left_ref[i] = whole.T.astype(BF16)
        back_ref[...] = carry_ref[...] if carry else jnp.zeros_like(back_ref)

    for first in range(0, moving_count, per):

        @pl.when(step == first // per)
        def _():
            for p, moving_ref in enumerate(moving_refs[first : first + per]):
                points = moving_ref[:feat, :]
                right_ref[p, :feat, :] = points
                right_ref[p, feat : 2 * feat, :] = points
                right_ref[p, 2 * feat :, :] = norm_rows(points, False).astype(BF16)
                dirs_ref[p] = moving_ref[feat:, :]

    span = range(0, rows, SUB)
    pairs = [(p, i) for p in range(per) for i in range(fixed_count)]
    if forward:
        tiles = [(p, i, c, r) for p, i in pairs for r in span for c in span]
    else:
        tiles = [(p, i, c, r) for p, i in pairs for c in span for r in span]
    squares, values, forward_sums, back_sums = {}, {}, {}, {}

    def add(sums, key, term):
        sums[key] = sums[key] + term if key in sums else term

    for t in range(len(tiles) + 2):
        if t < len(tiles):
            p, i, c, r = tiles[t]
            squares[t] = jnp.dot(
                left_ref[i, c : c + SUB, :depth],
                right_ref[p, :, r : r + SUB],
                preferred_element_type=F32,
            )
        if 1 <= t <= len(tiles):
            values[t - 1] = three_matern(squares.pop(t - 1))
        if t >= 2:
            p, i, c, r = tiles[t - 2]
            tile = values.pop(t - 2)
            if forward:
                dirs = fixed_refs[i][feat:, c : c + SUB]
                add(forward_sums, (p, r), jnp.dot(dirs, tile, preferred_element_type=F32))
            term = lax.dot_general(
                dirs_ref[p, :, r : r + SUB],
                tile,
                (((1,), (1,)), ((), ())),
                preferred_element_type=F32,
            )
            add(back_sums, (i, c), term)
    for (p, r), total in forward_sums.items():
        forward_ref[p, :, r : r + SUB] = (total * (1.0 / 3.0)).astype(forward_ref.dtype)
    for (i, c), total in back_sums.items():
        back_ref[i, :, c : c + SUB] += total * (1.0 / 3.0)


def tiles_call(fixed, moving, feat, per, forward=False, carry=None):
    fixed, moving = list(fixed), list(moving)
    height, rows = fixed[0].shape
    cols = height - feat
    depth = 2 * feat + NORM_ROWS
    whole = pl.BlockSpec((height, rows), lambda j: (0, 0))
    back_spec = pl.BlockSpec((len(fixed), cols, rows), lambda j: (0, 0, 0))
    out_shape, out_specs = [], []
    if forward:
        out_shape.append(jax.ShapeDtypeStruct((len(moving), cols, rows), BF16))
        out_specs.append(pl.BlockSpec((per, cols, rows), lambda j: (j, 0, 0)))
    out_shape.append(jax.ShapeDtypeStruct((len(fixed), cols, rows), F32))
    out_specs.append(back_spec)
    carried = [] if carry is None else [carry]
    evals = len(fixed) * len(moving) * rows * rows
    return pl.pallas_call(
        functools.partial(
            tiles_kernel, feat, len(fixed), len(moving), per, forward, bool(carried)
        ),
        grid=(len(moving) // per,),
        in_specs=[whole] * (len(fixed) + len(moving)) + [back_spec] * len(carried),
        out_specs=out_specs,
        out_shape=out_shape,
        scratch_shapes=[
            pltpu.VMEM((len(fixed), rows, 256), BF16),
            pltpu.VMEM((per, depth, rows), BF16),
            pltpu.VMEM((per, cols, rows), BF16),
        ],
        compiler_params=pltpu.CompilerParams(vmem_limit_bytes=40 * 2**20),
        cost_estimate=pl.CostEstimate(
            flops=2 * evals * 768,
            bytes_accessed=2 * height * rows * (len(moving) + len(fixed)),
            transcendentals=2 * evals,
        ),
    )(*fixed, *moving, *carried)


def pair_routes(mask, blocks, cores, reverse):
    routes = []
    for block in range(blocks):
        other = block ^ mask
        for core in range(cores):
            from_core = core if block < other else core ^ 1
            source, target = other * cores + from_core, block * cores + core
            routes.append((target, source) if reverse else (source, target))
    return routes


def over_pair(mask, array, reverse, beside=None):
    blocks, cores = lax.axis_size("blk"), lax.axis_size("core")

    def branch(known):
        def send(value, beside):
            swapped = None if beside is None else swap(beside, "yl")
            routes = pair_routes(known, blocks, cores, reverse)
            return lax.ppermute(value, ("blk", "core"), routes), swapped

        return send

    return lax.switch(mask - 1, [branch(known) for known in range(1, blocks)], array, beside)


def swap(array, axis, distance=1):
    return lax.ppermute(array, axis, [(i, i ^ distance) for i in range(lax.axis_size(axis))])


def shards(features, inv_scale, direction, residual, noise_variance, plan):
    feat = features.shape[1]
    rows, cols = direction.shape
    x_size = lax.axis_size("x")
    scaled = (features.astype(F32) * inv_scale).astype(BF16)
    packet = jnp.concatenate([scaled.T, direction.T], axis=0)

    def own_tiles(packets, carry=None):
        return tiles_call([packet], packets, feat, 2, carry=carry)[0]

    near = [packet] + [swap(packet, "x", shift) for shift in range(1, x_size)]
    partners = [over_pair(plan[r], packet, False)[0] for r in range(ROUNDS)]
    near_stack = jnp.stack(near)
    far_stack = swap(near_stack, "yl")
    near_forward, back = tiles_call(partners, near, feat, 1, forward=True)
    near_mates = swap(near_stack, "core")
    far_mates = swap(far_stack, "core")
    far = [far_stack[k] for k in range(x_size)]
    far_forward, back = tiles_call(partners, far, feat, 1, forward=True, carry=back)
    narrow_back = back.astype(BF16)
    first_back, arrived = over_pair(plan[0], narrow_back[0], True, far_forward)
    back_parts = [first_back]
    for r in range(1, ROUNDS):
        back_parts.append(over_pair(plan[r], narrow_back[r], True)[0])
    half = near_forward.astype(F32) + arrived.astype(F32)
    narrow_half = half.astype(BF16)
    total = half[0]
    for shift in range(1, x_size):
        total = total + swap(narrow_half[shift], "x", shift).astype(F32)
    own = own_tiles(near)
    own = own_tiles(far, own)
    mates = [stack[k] for stack in (near_mates, far_mates) for k in range(x_size)]
    own = own_tiles(mates, own)
    wide_dirs = direction.T.astype(F32)
    product = own[0] + total
    for part in back_parts:
        product = product + part.astype(F32)
    product = product + noise_variance[0] * wide_dirs
    inner = jnp.stack([jnp.sum(wide_dirs * product, axis=1), jnp.sum(residual.T * product, axis=1)])
    device_count = math.prod(lax.axis_size(axis) for axis in ALL)
    copies = jnp.broadcast_to(inner.reshape(1, 2 * cols), (device_count, 2 * cols))
    partials = lax.all_to_all(copies, ALL, 0, 0, tiled=True)
    totals = jnp.sum(partials, axis=0).reshape(2, cols)
    return (product.T, totals / (rows * device_count))


def solution(mesh):
    yl_size, cores = 2, 2
    groups = mesh.shape["sub"]
    split = mesh.devices.reshape(mesh.shape["blk"], yl_size, groups // (yl_size * cores), cores)
    by_rows = P(ALL, None)
    return jax.shard_map(
        shards,
        mesh=Mesh(split, ALL),
        in_specs=(by_rows, P(), by_rows, by_rows, P(), P()),
        out_specs=(by_rows, P()),
        check_vma=False,
    )
```

```python
import functools
import math

import jax
import jax.numpy as jnp
from jax import lax
from jax.experimental import pallas as pl
from jax.experimental.pallas import tpu as pltpu
from jax.sharding import Mesh, PartitionSpec as P

ROUNDS = 2
SUB = 256
NORM_ROWS = 16
LEFT_COLS = 256
VMEM_BYTES = 40 * 2**20
WIDTH = 1
LOG2E = math.log2(math.e)
F32 = jnp.float32
BF16 = jnp.bfloat16
ALL = ("blk", "yl", "x", "core")


def norm_rows(points, norms_first):
    wide = points.astype(F32)
    norms = 5.0 * jnp.sum(wide * wide, axis=0, keepdims=True)
    high = norms.astype(BF16).astype(F32)
    middle = (norms - high).astype(BF16).astype(F32)
    low = norms - high - middle
    row = lax.broadcasted_iota(jnp.int32, (NORM_ROWS, norms.shape[1]), 0)
    at, ones_at = (0, 3) if norms_first else (3, 0)
    rows = jnp.where((row >= ones_at) & (row < ones_at + 3), 1.0, 0.0)
    for offset, part in enumerate((high, middle, low)):
        rows = jnp.where(row == at + offset, part, rows)
    return rows


def three_matern(five_dist_sq):
    clipped = jnp.maximum(five_dist_sq, 1e-30)
    spread = clipped * lax.rsqrt(clipped)
    return ((clipped + (3.0 * spread + 3.0)) * jnp.exp2(spread * (-LOG2E))).astype(BF16)


def left_rows(packet, feat):
    points = packet[:feat, :]
    wide = points.astype(F32)
    pad = jnp.zeros((LEFT_COLS - 2 * feat - NORM_ROWS, points.shape[1]), F32)
    whole = jnp.concatenate([wide * -8.0, wide * -2.0, norm_rows(points, True), pad], axis=0)
    return whole.T.astype(BF16)


def right_rows(right_ref, p, points):
    feat = points.shape[0]
    right_ref[p, :feat, :] = points
    right_ref[p, feat : 2 * feat, :] = points
    right_ref[p, 2 * feat :, :] = norm_rows(points, False).astype(BF16)


def add(sums, key, term):
    sums[key] = sums[key] + term if key in sums else term


def run_tiles(tiles, left_of, right_of, use):
    squares, values = {}, {}
    for t in range(len(tiles) + 2):
        if t < len(tiles):
            left, right = left_of(tiles[t]), right_of(tiles[t])
            squares[t] = jnp.dot(left, right, preferred_element_type=F32)
        if 1 <= t <= len(tiles):
            values[t - 1] = three_matern(squares.pop(t - 1))
        if t >= 2:
            use(tiles[t - 2], values.pop(t - 2))


def times_transposed(dirs, tile):
    return lax.dot_general(dirs, tile, (((1,), (1,)), ((), ())), preferred_element_type=F32)


def pair_kernel(feat, carry, *refs):
    refs = list(refs)
    fixed_refs = [refs.pop(0) for _ in range(ROUNDS)]
    moving_ref = refs.pop(0)
    carry_ref = refs.pop(0) if carry else None
    forward_ref, back_ref, left_ref, right_ref = refs
    rows = moving_ref.shape[2]
    depth = 2 * feat + NORM_ROWS

    @pl.when(pl.program_id(0) == 0)
    def _():
        for i, fixed_ref in enumerate(fixed_refs):
            left_ref[i] = left_rows(fixed_ref[...], feat)
        back_ref[...] = carry_ref[...] if carry else jnp.zeros_like(back_ref)

    right_rows(right_ref, 0, moving_ref[0, :feat, :])
    span = range(0, rows, SUB)
    tiles = [(i, c, r) for i in range(ROUNDS) for r in span for c in span]
    forward_sums, back_sums = {}, {}

    def use(place, tile):
        i, c, r = place
        dirs = fixed_refs[i][feat:, c : c + SUB]
        add(forward_sums, r, jnp.dot(dirs, tile, preferred_element_type=F32))
        add(back_sums, (i, c), times_transposed(moving_ref[0, feat:, r : r + SUB], tile))

    run_tiles(
        tiles,
        lambda place: left_ref[place[0], place[1] : place[1] + SUB, :depth],
        lambda place: right_ref[0, :, place[2] : place[2] + SUB],
        use,
    )
    for r, total in forward_sums.items():
        forward_ref[0, :, r : r + SUB] = (total * (1.0 / 3.0)).astype(forward_ref.dtype)
    for (i, c), total in back_sums.items():
        back_ref[i, :, c : c + SUB] += total * (1.0 / 3.0)


def cost(evals, products):
    return pl.CostEstimate(
        flops=2 * evals * 256 * products, bytes_accessed=evals // 16, transcendentals=2 * evals
    )


def pair_call(fixed, moving, feat, carry=None):
    count, height, rows = moving.shape
    cols = height - feat
    depth = 2 * feat + NORM_ROWS
    back_spec = pl.BlockSpec((ROUNDS, cols, rows), lambda j: (0, 0, 0))
    carried = [] if carry is None else [carry]
    return pl.pallas_call(
        functools.partial(pair_kernel, feat, bool(carried)),
        grid=(count,),
        in_specs=[pl.BlockSpec((height, rows), lambda j: (0, 0))] * ROUNDS
        + [pl.BlockSpec((1, height, rows), lambda j: (j, 0, 0))]
        + [back_spec] * len(carried),
        out_specs=[pl.BlockSpec((1, cols, rows), lambda j: (j, 0, 0)), back_spec],
        out_shape=[
            jax.ShapeDtypeStruct((count, cols, rows), BF16),
            jax.ShapeDtypeStruct((ROUNDS, cols, rows), F32),
        ],
        scratch_shapes=[
            pltpu.VMEM((ROUNDS, rows, LEFT_COLS), BF16),
            pltpu.VMEM((1, depth, rows), BF16),
        ],
        compiler_params=pltpu.CompilerParams(vmem_limit_bytes=VMEM_BYTES),
        cost_estimate=cost(ROUNDS * count * rows * rows, 3),
    )(*fixed, moving, *carried)


def own_kernel(feat, parts, left_ref, *refs):
    moving_refs = refs[: len(parts)]
    carry_ref, back_ref, right_ref, dirs_ref = refs[len(parts) :]
    rows = right_ref.shape[2]
    depth = 2 * feat + NORM_ROWS
    step = pl.program_id(0)

    @pl.when(step == 0)
    def _():
        back_ref[...] = carry_ref[...]

    start = 0
    for count, moving_ref in zip(parts, moving_refs):

        @pl.when((step >= start) & (step < start + count))
        def _(moving_ref=moving_ref):
            right_rows(right_ref, 0, moving_ref[0, :feat, :])
            dirs_ref[...] = moving_ref[0, feat:, :]

        start += count
    span = range(0, rows, SUB)
    back_sums = {}

    def use(place, tile):
        c, r = place
        add(back_sums, c, times_transposed(dirs_ref[:, r : r + SUB], tile))

    run_tiles(
        [(c, r) for c in span for r in span],
        lambda place: left_ref[place[0] : place[0] + SUB, :depth],
        lambda place: right_ref[0, :, place[1] : place[1] + SUB],
        use,
    )
    for c, total in back_sums.items():
        back_ref[:, c : c + SUB] += total * (1.0 / 3.0)


def own_call(left, parts, carry, feat):
    _, height, rows = parts[0][0].shape
    cols = height - feat
    counts = [count for _, _, count in parts]
    steps = sum(counts)

    def block(start, first, count):
        return lambda j: (first + jnp.clip(j - start, 0, count - 1), 0, 0)

    moving_specs = [
        pl.BlockSpec((1, height, rows), block(sum(counts[:k]), first, count))
        for k, (_, first, count) in enumerate(parts)
    ]
    return pl.pallas_call(
        functools.partial(own_kernel, feat, counts),
        grid=(steps,),
        in_specs=[pl.BlockSpec(left.shape, lambda j: (0, 0))]
        + moving_specs
        + [pl.BlockSpec((cols, rows), lambda j: (0, 0))],
        out_specs=pl.BlockSpec((cols, rows), lambda j: (0, 0)),
        out_shape=jax.ShapeDtypeStruct((cols, rows), F32),
        scratch_shapes=[
            pltpu.VMEM((1, 2 * feat + NORM_ROWS, rows), BF16),
            pltpu.VMEM((cols, rows), BF16),
        ],
        compiler_params=pltpu.CompilerParams(vmem_limit_bytes=VMEM_BYTES),
        cost_estimate=cost(steps * rows * rows, 2),
    )(left, *[moving for moving, _, _ in parts], carry)


def short_kernel(feat, first, count, width, left_ref, moving_ref, carry_ref, back_ref, right_ref):
    rows = moving_ref.shape[2]
    depth = 2 * feat + NORM_ROWS
    steps = rows // (width * SUB)
    back_ref[...] = carry_ref[...]

    def prepare(p, _):
        right_rows(right_ref, p, moving_ref[first + p, :feat, :])
        return 0

    lax.fori_loop(0, count, prepare, 0)

    def step(at, _):
        p, start = at // steps, (at % steps) * (width * SUB)
        back_sums = {}

        def use(place, tile):
            c, r = place
            add(back_sums, c, times_transposed(moving_ref[first + p, feat:, r : r + SUB], tile))

        run_tiles(
            [(c * SUB, r) for c in range(width) for r in range(0, rows, SUB)],
            lambda place: left_ref[pl.ds(pl.multiple_of(start + place[0], SUB), SUB), :depth],
            lambda place: right_ref[p, :, place[1] : place[1] + SUB],
            use,
        )
        for c, total in back_sums.items():
            span = pl.ds(pl.multiple_of(start + c, SUB), SUB)
            back_ref[:, span] += total * (1.0 / 3.0)
        return 0

    lax.fori_loop(0, count * steps, step, 0)


def short_call(left, moving, carry, feat, first, count, width=WIDTH):
    _, height, rows = moving.shape
    return pl.pallas_call(
        functools.partial(short_kernel, feat, first, count, width),
        out_shape=jax.ShapeDtypeStruct((height - feat, rows), F32),
        scratch_shapes=[pltpu.VMEM((count, 2 * feat + NORM_ROWS, rows), BF16)],
        compiler_params=pltpu.CompilerParams(vmem_limit_bytes=VMEM_BYTES),
        cost_estimate=cost(count * rows * rows, 2),
    )(left, moving, carry)


def left_call(packet, feat):
    def kernel(packet_ref, left_ref):
        left_ref[...] = left_rows(packet_ref[...], feat)

    return pl.pallas_call(
        kernel, out_shape=jax.ShapeDtypeStruct((packet.shape[1], LEFT_COLS), BF16)
    )(packet)


def pair_routes(mask, blocks, cores):
    routes = []
    for block in range(blocks):
        other = block ^ mask
        for core in range(cores):
            from_core = core if block < other else core ^ 1
            routes.append((other * cores + from_core, block * cores + core))
    return routes


def over_pair(mask, array, work, *operands):
    blocks, cores = lax.axis_size("blk"), lax.axis_size("core")

    def branch(known):
        def send(value, *operands):
            routes = pair_routes(known, blocks, cores)
            return lax.ppermute(value, ("blk", "core"), routes), work(*operands)

        return send

    return lax.switch(mask - 1, [branch(known) for known in range(1, blocks)], array, *operands)


def swap(array, axis, distance=1):
    return lax.ppermute(array, axis, [(i, i ^ distance) for i in range(lax.axis_size(axis))])


def shards(features, inv_scale, direction, residual, noise_variance, plan):
    feat = features.shape[1]
    rows, cols = direction.shape
    x_size = lax.axis_size("x")
    scaled = (features.astype(F32) * inv_scale).astype(BF16)
    packet = jnp.concatenate([scaled.T, direction.T], axis=0)

    def short(first, count):
        return lambda left, moving, carry: short_call(left, moving, carry, feat, first, count)

    def own_tiles(own, *parts):
        return own_call(left, list(parts), own, feat)

    left = left_call(packet, feat)
    near = [packet] + [swap(packet, "x", shift) for shift in range(1, x_size)]
    own = jnp.zeros((cols, rows), F32)
    first_partner, own = over_pair(plan[0], packet, short(0, 1), left, packet[None], own)
    near = jnp.stack(near)
    second_partner, own = over_pair(plan[1], packet, short(1, 2), left, near, own)
    near, second_partner = lax.optimization_barrier((near, second_partner))
    partners = [first_partner, second_partner]
    far = swap(near, "yl")
    near_mates = swap(near, "core")
    near_forward, back = pair_call(partners, near, feat)
    own = own_tiles(own, (near, 3, 1), (near_mates, 0, 2))
    far, own = lax.optimization_barrier((far, own))
    far_mates = swap(far, "core")
    far_forward, back = pair_call(partners, far, feat, back)

    masks = plan[:ROUNDS]
    position = lax.axis_index("blk")
    follower = position > jnp.bitwise_xor(position, masks)

    def back_step(back, own, axis, distance, taken, *parts):
        arrived = swap(back, axis, distance)
        own = own_tiles(own, *parts)
        back = jnp.where(taken[:, None, None], arrived, back)
        return lax.optimization_barrier((back, own))

    def bit(at):
        return jnp.bitwise_and(jnp.right_shift(masks, at), 1) == 1

    sums = jnp.stack([near_forward, far_forward])
    back = back.astype(BF16)
    back, own = back_step(back, own, "core", 1, follower, (near_mates, 2, 2))
    back, own = back_step(back, own, "blk", 1, bit(0), (far, 0, 2))
    halves = sums[:, 0].astype(F32)
    for shift in range(1, x_size):
        halves = halves + swap(sums[:, shift], "x", shift).astype(F32)
    halves, own = lax.optimization_barrier((halves, own))
    total = halves[0] + swap(halves[1].astype(BF16), "yl").astype(F32)
    back, own = back_step(back, own, "blk", 2, bit(1), (far, 2, 2), (far_mates, 0, 1))
    back, own = back_step(back, own, "blk", 4, bit(2), (far_mates, 1, 3))
    wide_dirs = direction.T.astype(F32)
    product = own + total + jnp.sum(back.astype(F32), axis=0)
    product = product + noise_variance[0] * wide_dirs
    inner = jnp.stack([jnp.sum(wide_dirs * product, axis=1), jnp.sum(residual.T * product, axis=1)])
    device_count = math.prod(lax.axis_size(axis) for axis in ALL)
    copies = jnp.broadcast_to(inner.reshape(1, 2 * cols), (device_count, 2 * cols))
    partials = lax.all_to_all(copies, ALL, 0, 0, tiled=True)
    totals = jnp.sum(partials, axis=0).reshape(2, cols)
    return (product.T, totals / (rows * device_count))


def solution(mesh):
    yl_size, cores = 2, 2
    groups = mesh.shape["sub"]
    split = mesh.devices.reshape(mesh.shape["blk"], yl_size, groups // (yl_size * cores), cores)
    by_rows = P(ALL, None)
    return jax.shard_map(
        shards,
        mesh=Mesh(split, ALL),
        in_specs=(by_rows, P(), by_rows, by_rows, P(), P()),
        out_specs=(by_rows, P()),
        check_vma=False,
    )
```

```python
import functools
import math

import jax
import jax.numpy as jnp
from jax import lax
from jax.experimental import pallas as pl
from jax.experimental.pallas import tpu as pltpu
from jax.sharding import Mesh, PartitionSpec as P

ROUNDS = 2
SUB = 256
NORM_ROWS = 16
LEFT_COLS = 256
VMEM_BYTES = 40 * 2**20
WIDTH = 1
LOG2E = math.log2(math.e)
F32 = jnp.float32
BF16 = jnp.bfloat16
ALL = ("blk", "yl", "x", "core")


def norm_rows(points, norms_first):
    wide = points.astype(F32)
    norms = 5.0 * jnp.sum(wide * wide, axis=0, keepdims=True)
    high = norms.astype(BF16).astype(F32)
    middle = (norms - high).astype(BF16).astype(F32)
    low = norms - high - middle
    row = lax.broadcasted_iota(jnp.int32, (NORM_ROWS, norms.shape[1]), 0)
    at, ones_at = (0, 3) if norms_first else (3, 0)
    rows = jnp.where((row >= ones_at) & (row < ones_at + 3), 1.0, 0.0)
    for offset, part in enumerate((high, middle, low)):
        rows = jnp.where(row == at + offset, part, rows)
    return rows


def three_matern(five_dist_sq):
    clipped = jnp.maximum(five_dist_sq, 1e-30)
    spread = clipped * lax.rsqrt(clipped)
    return ((clipped + (3.0 * spread + 3.0)) * jnp.exp2(spread * (-LOG2E))).astype(BF16)


def left_rows(packet, feat):
    points = packet[:feat, :]
    wide = points.astype(F32)
    pad = jnp.zeros((LEFT_COLS - 2 * feat - NORM_ROWS, points.shape[1]), F32)
    whole = jnp.concatenate([wide * -8.0, wide * -2.0, norm_rows(points, True), pad], axis=0)
    return whole.T.astype(BF16)


def right_rows(right_ref, p, points):
    feat = points.shape[0]
    right_ref[p, :feat, :] = points
    right_ref[p, feat : 2 * feat, :] = points
    right_ref[p, 2 * feat :, :] = norm_rows(points, False).astype(BF16)


def add(sums, key, term):
    sums[key] = sums[key] + term if key in sums else term


def run_tiles(tiles, left_of, right_of, use):
    squares, values = {}, {}
    for t in range(len(tiles) + 2):
        if t < len(tiles):
            left, right = left_of(tiles[t]), right_of(tiles[t])
            squares[t] = jnp.dot(left, right, preferred_element_type=F32)
        if 1 <= t <= len(tiles):
            values[t - 1] = three_matern(squares.pop(t - 1))
        if t >= 2:
            use(tiles[t - 2], values.pop(t - 2))


def times_transposed(dirs, tile):
    return lax.dot_general(dirs, tile, (((1,), (1,)), ((), ())), preferred_element_type=F32)


def pair_kernel(feat, carry, *refs):
    refs = list(refs)
    fixed_refs = [refs.pop(0) for _ in range(ROUNDS)]
    moving_ref = refs.pop(0)
    carry_ref = refs.pop(0) if carry else None
    forward_ref, back_ref, left_ref, right_ref = refs
    rows = moving_ref.shape[2]
    depth = 2 * feat + NORM_ROWS

    @pl.when(pl.program_id(0) == 0)
    def _():
        for i, fixed_ref in enumerate(fixed_refs):
            left_ref[i] = left_rows(fixed_ref[...], feat)
        back_ref[...] = carry_ref[...] if carry else jnp.zeros_like(back_ref)

    right_rows(right_ref, 0, moving_ref[0, :feat, :])
    span = range(0, rows, SUB)
    tiles = [(i, c, r) for i in range(ROUNDS) for r in span for c in span]
    forward_sums, back_sums = {}, {}

    def use(place, tile):
        i, c, r = place
        dirs = fixed_refs[i][feat:, c : c + SUB]
        add(forward_sums, r, jnp.dot(dirs, tile, preferred_element_type=F32))
        add(back_sums, (i, c), times_transposed(moving_ref[0, feat:, r : r + SUB], tile))

    run_tiles(
        tiles,
        lambda place: left_ref[place[0], place[1] : place[1] + SUB, :depth],
        lambda place: right_ref[0, :, place[2] : place[2] + SUB],
        use,
    )
    for r, total in forward_sums.items():
        forward_ref[0, :, r : r + SUB] = (total * (1.0 / 3.0)).astype(forward_ref.dtype)
    for (i, c), total in back_sums.items():
        back_ref[i, :, c : c + SUB] += total * (1.0 / 3.0)


def cost(evals, products):
    return pl.CostEstimate(
        flops=2 * evals * 256 * products, bytes_accessed=evals // 16, transcendentals=2 * evals
    )


def pair_call(fixed, moving, feat, carry=None):
    count, height, rows = moving.shape
    cols = height - feat
    depth = 2 * feat + NORM_ROWS
    back_spec = pl.BlockSpec((ROUNDS, cols, rows), lambda j: (0, 0, 0))
    carried = [] if carry is None else [carry]
    return pl.pallas_call(
        functools.partial(pair_kernel, feat, bool(carried)),
        grid=(count,),
        in_specs=[pl.BlockSpec((height, rows), lambda j: (0, 0))] * ROUNDS
        + [pl.BlockSpec((1, height, rows), lambda j: (j, 0, 0))]
        + [back_spec] * len(carried),
        out_specs=[pl.BlockSpec((1, cols, rows), lambda j: (j, 0, 0)), back_spec],
        out_shape=[
            jax.ShapeDtypeStruct((count, cols, rows), BF16),
            jax.ShapeDtypeStruct((ROUNDS, cols, rows), F32),
        ],
        scratch_shapes=[
            pltpu.VMEM((ROUNDS, rows, LEFT_COLS), BF16),
            pltpu.VMEM((1, depth, rows), BF16),
        ],
        compiler_params=pltpu.CompilerParams(vmem_limit_bytes=VMEM_BYTES),
        cost_estimate=cost(ROUNDS * count * rows * rows, 3),
    )(*fixed, moving, *carried)


def own_kernel(feat, parts, left_ref, *refs):
    moving_refs = refs[: len(parts)]
    carry_ref, back_ref, right_ref, dirs_ref = refs[len(parts) :]
    rows = right_ref.shape[2]
    depth = 2 * feat + NORM_ROWS
    step = pl.program_id(0)

    @pl.when(step == 0)
    def _():
        back_ref[...] = carry_ref[...]

    start = 0
    for count, moving_ref in zip(parts, moving_refs):

        @pl.when((step >= start) & (step < start + count))
        def _(moving_ref=moving_ref):
            right_rows(right_ref, 0, moving_ref[0, :feat, :])
            dirs_ref[...] = moving_ref[0, feat:, :]

        start += count
    span = range(0, rows, SUB)
    back_sums = {}

    def use(place, tile):
        c, r = place
        add(back_sums, c, times_transposed(dirs_ref[:, r : r + SUB], tile))

    run_tiles(
        [(c, r) for c in span for r in span],
        lambda place: left_ref[place[0] : place[0] + SUB, :depth],
        lambda place: right_ref[0, :, place[1] : place[1] + SUB],
        use,
    )
    for c, total in back_sums.items():
        back_ref[:, c : c + SUB] += total * (1.0 / 3.0)


def own_call(left, parts, carry, feat):
    _, height, rows = parts[0][0].shape
    cols = height - feat
    counts = [count for _, _, count in parts]
    steps = sum(counts)

    def block(start, first, count):
        return lambda j: (first + jnp.clip(j - start, 0, count - 1), 0, 0)

    moving_specs = [
        pl.BlockSpec((1, height, rows), block(sum(counts[:k]), first, count))
        for k, (_, first, count) in enumerate(parts)
    ]
    return pl.pallas_call(
        functools.partial(own_kernel, feat, counts),
        grid=(steps,),
        in_specs=[pl.BlockSpec(left.shape, lambda j: (0, 0))]
        + moving_specs
        + [pl.BlockSpec((cols, rows), lambda j: (0, 0))],
        out_specs=pl.BlockSpec((cols, rows), lambda j: (0, 0)),
        out_shape=jax.ShapeDtypeStruct((cols, rows), F32),
        scratch_shapes=[
            pltpu.VMEM((1, 2 * feat + NORM_ROWS, rows), BF16),
            pltpu.VMEM((cols, rows), BF16),
        ],
        compiler_params=pltpu.CompilerParams(vmem_limit_bytes=VMEM_BYTES),
        cost_estimate=cost(steps * rows * rows, 2),
    )(left, *[moving for moving, _, _ in parts], carry)


def short_kernel(feat, first, count, width, left_ref, moving_ref, carry_ref, back_ref, right_ref):
    rows = moving_ref.shape[2]
    depth = 2 * feat + NORM_ROWS
    steps = rows // (width * SUB)
    back_ref[...] = carry_ref[...]

    def prepare(p, _):
        right_rows(right_ref, p, moving_ref[first + p, :feat, :])
        return 0

    lax.fori_loop(0, count, prepare, 0)

    def step(at, _):
        p, start = at // steps, (at % steps) * (width * SUB)
        back_sums = {}

        def use(place, tile):
            c, r = place
            add(back_sums, c, times_transposed(moving_ref[first + p, feat:, r : r + SUB], tile))

        run_tiles(
            [(c * SUB, r) for c in range(width) for r in range(0, rows, SUB)],
            lambda place: left_ref[pl.ds(pl.multiple_of(start + place[0], SUB), SUB), :depth],
            lambda place: right_ref[p, :, place[1] : place[1] + SUB],
            use,
        )
        for c, total in back_sums.items():
            span = pl.ds(pl.multiple_of(start + c, SUB), SUB)
            back_ref[:, span] += total * (1.0 / 3.0)
        return 0

    lax.fori_loop(0, count * steps, step, 0)


def short_call(left, moving, carry, feat, first, count, width=WIDTH):
    _, height, rows = moving.shape
    return pl.pallas_call(
        functools.partial(short_kernel, feat, first, count, width),
        out_shape=jax.ShapeDtypeStruct((height - feat, rows), F32),
        scratch_shapes=[pltpu.VMEM((count, 2 * feat + NORM_ROWS, rows), BF16)],
        compiler_params=pltpu.CompilerParams(vmem_limit_bytes=VMEM_BYTES),
        cost_estimate=cost(count * rows * rows, 2),
    )(left, moving, carry)


def left_call(packet, feat):
    def kernel(packet_ref, left_ref):
        left_ref[...] = left_rows(packet_ref[...], feat)

    return pl.pallas_call(
        kernel, out_shape=jax.ShapeDtypeStruct((packet.shape[1], LEFT_COLS), BF16)
    )(packet)


def pair_routes(mask, blocks, cores):
    routes = []
    for block in range(blocks):
        other = block ^ mask
        for core in range(cores):
            from_core = core if block < other else core ^ 1
            routes.append((other * cores + from_core, block * cores + core))
    return routes


def over_pair(mask, array, work, *operands):
    blocks, cores = lax.axis_size("blk"), lax.axis_size("core")

    def branch(known):
        def send(value, *operands):
            routes = pair_routes(known, blocks, cores)
            return lax.ppermute(value, ("blk", "core"), routes), work(*operands)

        return send

    return lax.switch(mask - 1, [branch(known) for known in range(1, blocks)], array, *operands)


def swap(array, axis, distance=1):
    return lax.ppermute(array, axis, [(i, i ^ distance) for i in range(lax.axis_size(axis))])


def shards(features, inv_scale, direction, residual, noise_variance, plan):
    feat = features.shape[1]
    rows, cols = direction.shape
    x_size = lax.axis_size("x")
    scaled = (features.astype(F32) * inv_scale).astype(BF16)
    packet = jnp.concatenate([scaled.T, direction.T], axis=0)

    def short(first, count):
        return lambda left, moving, carry: short_call(left, moving, carry, feat, first, count)

    def own_tiles(own, *parts):
        return own_call(left, list(parts), own, feat)

    left = left_call(packet, feat)
    near = [packet] + [swap(packet, "x", shift) for shift in range(1, x_size)]
    own = jnp.zeros((cols, rows), F32)
    first_partner, own = over_pair(plan[0], packet, short(0, 1), left, packet[None], own)
    near = jnp.stack(near)
    second_partner, own = over_pair(plan[1], packet, short(1, 2), left, near, own)
    near, second_partner = lax.optimization_barrier((near, second_partner))
    partners = [first_partner, second_partner]
    far = swap(near, "yl")
    near_mates = swap(near, "core")
    near_forward, back = pair_call(partners, near, feat)
    own = own_tiles(own, (near, 3, 1), (near_mates, 0, 2))
    far, own = lax.optimization_barrier((far, own))
    far_mates = swap(far, "core")
    far_forward, back = pair_call(partners, far, feat, back)

    masks = plan[:ROUNDS]
    position = lax.axis_index("blk")
    follower = position > jnp.bitwise_xor(position, masks)

    def taken(at):
        return jnp.bitwise_and(jnp.right_shift(masks, at), 1)[:, None, None] == 1

    sums = jnp.stack([near_forward, far_forward])
    back = back.astype(BF16)
    arrived = swap(back, "core")
    shares = [swap(sums[:, shift], "x", shift) for shift in range(1, x_size)]
    own = own_tiles(own, (near_mates, 2, x_size - 2), (far, 0, 1))
    arrived, own = lax.optimization_barrier((arrived, own))
    back = jnp.where(follower[:, None, None], arrived, back)

    arrived = swap(back, "blk", 1)
    own = own_tiles(own, (far, 1, x_size - 1))
    arrived, shares, own = lax.optimization_barrier((arrived, shares, own))
    back = jnp.where(taken(0), arrived, back)
    halves = sums[:, 0].astype(F32)
    for share in shares:
        halves = halves + share.astype(F32)

    arrived = [swap(back, "blk", distance) for distance in (2, 4, 6)]
    share = swap(halves[1].astype(BF16), "yl")
    own = own_tiles(own, (far_mates, 0, x_size))
    (one, two, both), share, own = lax.optimization_barrier((arrived, share, own))
    total = halves[0] + share.astype(F32)
    back = jnp.where(taken(2), jnp.where(taken(1), both, two), jnp.where(taken(1), one, back))
    wide_dirs = direction.T.astype(F32)
    product = own + total + jnp.sum(back.astype(F32), axis=0)
    product = product + noise_variance[0] * wide_dirs
    inner = jnp.stack([jnp.sum(wide_dirs * product, axis=1), jnp.sum(residual.T * product, axis=1)])
    device_count = math.prod(lax.axis_size(axis) for axis in ALL)
    copies = jnp.broadcast_to(inner.reshape(1, 2 * cols), (device_count, 2 * cols))
    partials = lax.all_to_all(copies, ALL, 0, 0, tiled=True)
    totals = jnp.sum(partials, axis=0).reshape(2, cols)
    return (product.T, totals / (rows * device_count))


def solution(mesh):
    yl_size, cores = 2, 2
    groups = mesh.shape["sub"]
    split = mesh.devices.reshape(mesh.shape["blk"], yl_size, groups // (yl_size * cores), cores)
    by_rows = P(ALL, None)
    return jax.shard_map(
        shards,
        mesh=Mesh(split, ALL),
        in_specs=(by_rows, P(), by_rows, by_rows, P(), P()),
        out_specs=(by_rows, P()),
        check_vma=False,
    )
```

```python
import functools
import math

import jax
import jax.numpy as jnp
from jax import lax
from jax.experimental import pallas as pl
from jax.experimental.pallas import tpu as pltpu
from jax.sharding import Mesh, PartitionSpec as P

ROUNDS = 2
SUB = 256
NORM_ROWS = 16
LEFT_COLS = 256
VMEM_BYTES = 40 * 2**20
LOG2E = math.log2(math.e)
F32 = jnp.float32
BF16 = jnp.bfloat16
ALL = ("blk", "yl", "x", "core")


def norm_rows(points, norms_first):
    wide = points.astype(F32)
    norms = 5.0 * jnp.sum(wide * wide, axis=0, keepdims=True)
    high = norms.astype(BF16).astype(F32)
    middle = (norms - high).astype(BF16).astype(F32)
    low = norms - high - middle
    row = lax.broadcasted_iota(jnp.int32, (NORM_ROWS, norms.shape[1]), 0)
    at, ones_at = (0, 3) if norms_first else (3, 0)
    rows = jnp.where((row >= ones_at) & (row < ones_at + 3), 1.0, 0.0)
    for offset, part in enumerate((high, middle, low)):
        rows = jnp.where(row == at + offset, part, rows)
    return rows


def three_matern(five_dist_sq):
    clipped = jnp.maximum(five_dist_sq, 1e-30)
    spread = clipped * lax.rsqrt(clipped)
    return ((clipped + (3.0 * spread + 3.0)) * jnp.exp2(spread * (-LOG2E))).astype(BF16)


def left_rows(packet, feat):
    points = packet[:feat, :]
    wide = points.astype(F32)
    pad = jnp.zeros((LEFT_COLS - 2 * feat - NORM_ROWS, points.shape[1]), F32)
    whole = jnp.concatenate([wide * -8.0, wide * -2.0, norm_rows(points, True), pad], axis=0)
    return whole.T.astype(BF16)


def right_rows(right_ref, p, points):
    feat = points.shape[0]
    right_ref[p, :feat, :] = points
    right_ref[p, feat : 2 * feat, :] = points
    right_ref[p, 2 * feat :, :] = norm_rows(points, False).astype(BF16)


def add(sums, key, term):
    sums[key] = sums[key] + term if key in sums else term


def run_tiles(tiles, left_of, right_of, use):
    squares, values = {}, {}
    for t in range(len(tiles) + 2):
        if t < len(tiles):
            left, right = left_of(tiles[t]), right_of(tiles[t])
            squares[t] = jnp.dot(left, right, preferred_element_type=F32)
        if 1 <= t <= len(tiles):
            values[t - 1] = three_matern(squares.pop(t - 1))
        if t >= 2:
            use(tiles[t - 2], values.pop(t - 2))


def times_transposed(dirs, tile):
    return lax.dot_general(dirs, tile, (((1,), (1,)), ((), ())), preferred_element_type=F32)


def pair_kernel(feat, carry, *refs):
    refs = list(refs)
    fixed_refs = [refs.pop(0) for _ in range(ROUNDS)]
    moving_ref = refs.pop(0)
    carry_ref = refs.pop(0) if carry else None
    forward_ref, back_ref, left_ref, right_ref = refs
    rows = moving_ref.shape[2]
    depth = 2 * feat + NORM_ROWS

    @pl.when(pl.program_id(0) == 0)
    def _():
        for i, fixed_ref in enumerate(fixed_refs):
            left_ref[i] = left_rows(fixed_ref[...], feat)
        back_ref[...] = carry_ref[...] if carry else jnp.zeros_like(back_ref)

    right_rows(right_ref, 0, moving_ref[0, :feat, :])
    span = range(0, rows, SUB)
    tiles = [(i, c, r) for i in range(ROUNDS) for r in span for c in span]
    forward_sums, back_sums = {}, {}

    def use(place, tile):
        i, c, r = place
        dirs = fixed_refs[i][feat:, c : c + SUB]
        add(forward_sums, r, jnp.dot(dirs, tile, preferred_element_type=F32))
        add(back_sums, (i, c), times_transposed(moving_ref[0, feat:, r : r + SUB], tile))

    run_tiles(
        tiles,
        lambda place: left_ref[place[0], place[1] : place[1] + SUB, :depth],
        lambda place: right_ref[0, :, place[2] : place[2] + SUB],
        use,
    )
    for r, total in forward_sums.items():
        forward_ref[0, :, r : r + SUB] = (total * (1.0 / 3.0)).astype(forward_ref.dtype)
    for (i, c), total in back_sums.items():
        back_ref[i, :, c : c + SUB] += total * (1.0 / 3.0)


def cost(evals, products):
    return pl.CostEstimate(
        flops=2 * evals * 256 * products, bytes_accessed=evals // 16, transcendentals=2 * evals
    )


def pair_call(fixed, moving, feat, carry=None):
    count, height, rows = moving.shape
    cols = height - feat
    depth = 2 * feat + NORM_ROWS
    back_spec = pl.BlockSpec((ROUNDS, cols, rows), lambda j: (0, 0, 0))
    carried = [] if carry is None else [carry]
    return pl.pallas_call(
        functools.partial(pair_kernel, feat, bool(carried)),
        grid=(count,),
        in_specs=[pl.BlockSpec((height, rows), lambda j: (0, 0))] * ROUNDS
        + [pl.BlockSpec((1, height, rows), lambda j: (j, 0, 0))]
        + [back_spec] * len(carried),
        out_specs=[pl.BlockSpec((1, cols, rows), lambda j: (j, 0, 0)), back_spec],
        out_shape=[
            jax.ShapeDtypeStruct((count, cols, rows), BF16),
            jax.ShapeDtypeStruct((ROUNDS, cols, rows), F32),
        ],
        scratch_shapes=[
            pltpu.VMEM((ROUNDS, rows, LEFT_COLS), BF16),
            pltpu.VMEM((1, depth, rows), BF16),
        ],
        compiler_params=pltpu.CompilerParams(vmem_limit_bytes=VMEM_BYTES),
        cost_estimate=cost(ROUNDS * count * rows * rows, 3),
    )(*fixed, moving, *carried)


def own_kernel(feat, parts, left_ref, *refs):
    moving_refs = refs[: len(parts)]
    carry_ref, back_ref, right_ref, dirs_ref = refs[len(parts) :]
    rows = right_ref.shape[2]
    depth = 2 * feat + NORM_ROWS
    step = pl.program_id(0)

    @pl.when(step == 0)
    def _():
        back_ref[...] = carry_ref[...]

    start = 0
    for count, moving_ref in zip(parts, moving_refs):

        @pl.when((step >= start) & (step < start + count))
        def _(moving_ref=moving_ref):
            right_rows(right_ref, 0, moving_ref[0, :feat, :])
            dirs_ref[...] = moving_ref[0, feat:, :]

        start += count
    span = range(0, rows, SUB)
    back_sums = {}

    def use(place, tile):
        c, r = place
        add(back_sums, c, times_transposed(dirs_ref[:, r : r + SUB], tile))

    run_tiles(
        [(c, r) for c in span for r in span],
        lambda place: left_ref[place[0] : place[0] + SUB, :depth],
        lambda place: right_ref[0, :, place[1] : place[1] + SUB],
        use,
    )
    for c, total in back_sums.items():
        back_ref[:, c : c + SUB] += total * (1.0 / 3.0)


def own_call(left, parts, carry, feat):
    _, height, rows = parts[0][0].shape
    cols = height - feat
    counts = [count for _, _, count in parts]
    steps = sum(counts)

    def block(start, first, count):
        return lambda j: (first + jnp.clip(j - start, 0, count - 1), 0, 0)

    moving_specs = [
        pl.BlockSpec((1, height, rows), block(sum(counts[:k]), first, count))
        for k, (_, first, count) in enumerate(parts)
    ]
    return pl.pallas_call(
        functools.partial(own_kernel, feat, counts),
        grid=(steps,),
        in_specs=[pl.BlockSpec(left.shape, lambda j: (0, 0))]
        + moving_specs
        + [pl.BlockSpec((cols, rows), lambda j: (0, 0))],
        out_specs=pl.BlockSpec((cols, rows), lambda j: (0, 0)),
        out_shape=jax.ShapeDtypeStruct((cols, rows), F32),
        scratch_shapes=[
            pltpu.VMEM((1, 2 * feat + NORM_ROWS, rows), BF16),
            pltpu.VMEM((cols, rows), BF16),
        ],
        compiler_params=pltpu.CompilerParams(vmem_limit_bytes=VMEM_BYTES),
        cost_estimate=cost(steps * rows * rows, 2),
    )(left, *[moving for moving, _, _ in parts], carry)


def short_kernel(feat, first, count, width, left_ref, moving_ref, carry_ref, back_ref, right_ref):
    rows = moving_ref.shape[2]
    depth = 2 * feat + NORM_ROWS
    steps = rows // (width * SUB)
    back_ref[...] = carry_ref[...]

    def prepare(p, _):
        right_rows(right_ref, p, moving_ref[first + p, :feat, :])
        return 0

    lax.fori_loop(0, count, prepare, 0)

    def step(at, _):
        p, start = at // steps, (at % steps) * (width * SUB)
        back_sums = {}

        def use(place, tile):
            c, r = place
            add(back_sums, c, times_transposed(moving_ref[first + p, feat:, r : r + SUB], tile))

        run_tiles(
            [(c * SUB, r) for c in range(width) for r in range(0, rows, SUB)],
            lambda place: left_ref[pl.ds(pl.multiple_of(start + place[0], SUB), SUB), :depth],
            lambda place: right_ref[p, :, place[1] : place[1] + SUB],
            use,
        )
        for c, total in back_sums.items():
            span = pl.ds(pl.multiple_of(start + c, SUB), SUB)
            back_ref[:, span] += total * (1.0 / 3.0)
        return 0

    lax.fori_loop(0, count * steps, step, 0)


def short_call(left, moving, carry, feat, first, count, width):
    _, height, rows = moving.shape
    return pl.pallas_call(
        functools.partial(short_kernel, feat, first, count, width),
        out_shape=jax.ShapeDtypeStruct((height - feat, rows), F32),
        scratch_shapes=[pltpu.VMEM((count, 2 * feat + NORM_ROWS, rows), BF16)],
        compiler_params=pltpu.CompilerParams(vmem_limit_bytes=VMEM_BYTES),
        cost_estimate=cost(count * rows * rows, 2),
    )(left, moving, carry)


def left_call(packet, feat):
    def kernel(packet_ref, left_ref):
        left_ref[...] = left_rows(packet_ref[...], feat)

    return pl.pallas_call(
        kernel, out_shape=jax.ShapeDtypeStruct((packet.shape[1], LEFT_COLS), BF16)
    )(packet)


def pair_routes(mask, blocks, cores):
    routes = []
    for block in range(blocks):
        other = block ^ mask
        for core in range(cores):
            from_core = core if block < other else core ^ 1
            routes.append((other * cores + from_core, block * cores + core))
    return routes


def over_pair(mask, array, work, *operands):
    blocks, cores = lax.axis_size("blk"), lax.axis_size("core")

    def branch(known):
        def send(value, *operands):
            routes = pair_routes(known, blocks, cores)
            return lax.ppermute(value, ("blk", "core"), routes), work(*operands)

        return send

    return lax.switch(mask - 1, [branch(known) for known in range(1, blocks)], array, *operands)


def swap(array, axis, distance=1):
    return lax.ppermute(array, axis, [(i, i ^ distance) for i in range(lax.axis_size(axis))])


def shards(features, inv_scale, direction, residual, noise_variance, plan):
    feat = features.shape[1]
    rows, cols = direction.shape
    x_size = lax.axis_size("x")
    scaled = (features.astype(F32) * inv_scale).astype(BF16)
    packet = jnp.concatenate([scaled.T, direction.T], axis=0)

    def short(first, count, width):
        return lambda left, moving, carry: short_call(left, moving, carry, feat, first, count, width)

    def own_tiles(own, *parts):
        return own_call(left, list(parts), own, feat)

    left = left_call(packet, feat)
    near = [packet] + [swap(packet, "x", shift) for shift in range(1, x_size)]
    own = jnp.zeros((cols, rows), F32)
    first_partner, own = over_pair(plan[0], packet, short(0, 1, 1), left, packet[None], own)
    near = jnp.stack(near)
    second_partner, own = over_pair(plan[1], packet, short(1, 3, 2), left, near, own)
    near, second_partner = lax.optimization_barrier((near, second_partner))
    partners = [first_partner, second_partner]
    far = swap(near, "yl")
    near_mates = swap(near, "core")
    near_forward, back = pair_call(partners, near, feat)
    own = own_tiles(own, (near_mates, 0, 2))
    far, own = lax.optimization_barrier((far, own))
    far_mates = swap(far, "core")
    far_forward, back = pair_call(partners, far, feat, back)

    masks = plan[:ROUNDS]
    position = lax.axis_index("blk")
    follower = position > jnp.bitwise_xor(position, masks)

    def taken(at):
        return jnp.bitwise_and(jnp.right_shift(masks, at), 1)[:, None, None] == 1

    sums = jnp.stack([near_forward, far_forward])
    back = back.astype(BF16)
    arrived = swap(back, "core")
    shares = [swap(sums[:, shift], "x", shift) for shift in range(1, x_size)]
    own = own_tiles(own, (near_mates, 2, x_size - 2), (far, 0, 1))
    arrived, own = lax.optimization_barrier((arrived, own))
    back = jnp.where(follower[:, None, None], arrived, back)

    arrived = swap(back, "blk", 1)
    own = own_tiles(own, (far, 1, x_size - 1))
    arrived, shares, own = lax.optimization_barrier((arrived, shares, own))
    back = jnp.where(taken(0), arrived, back)
    halves = sums[:, 0].astype(F32)
    for share in shares:
        halves = halves + share.astype(F32)

    arrived = [swap(back, "blk", distance) for distance in (2, 4, 6)]
    share = swap(halves[1].astype(BF16), "yl")
    own = own_tiles(own, (far_mates, 0, x_size))
    (one, two, both), share, own = lax.optimization_barrier((arrived, share, own))
    total = halves[0] + share.astype(F32)
    back = jnp.where(taken(2), jnp.where(taken(1), both, two), jnp.where(taken(1), one, back))
    wide_dirs = direction.T.astype(F32)
    product = own + total + jnp.sum(back.astype(F32), axis=0)
    product = product + noise_variance[0] * wide_dirs
    inner = jnp.stack([jnp.sum(wide_dirs * product, axis=1), jnp.sum(residual.T * product, axis=1)])
    device_count = math.prod(lax.axis_size(axis) for axis in ALL)
    copies = jnp.broadcast_to(inner.reshape(1, 2 * cols), (device_count, 2 * cols))
    partials = lax.all_to_all(copies, ALL, 0, 0, tiled=True)
    totals = jnp.sum(partials, axis=0).reshape(2, cols)
    return (product.T, totals / (rows * device_count))


def solution(mesh):
    yl_size, cores = 2, 2
    groups = mesh.shape["sub"]
    split = mesh.devices.reshape(mesh.shape["blk"], yl_size, groups // (yl_size * cores), cores)
    by_rows = P(ALL, None)
    return jax.shard_map(
        shards,
        mesh=Mesh(split, ALL),
        in_specs=(by_rows, P(), by_rows, by_rows, P(), P()),
        out_specs=(by_rows, P()),
        check_vma=False,
    )
```

```python
import functools
import math

import jax
import jax.numpy as jnp
from jax import lax
from jax.experimental import pallas as pl
from jax.experimental.pallas import tpu as pltpu
from jax.sharding import Mesh, PartitionSpec as P

ROUNDS = 2
SUB = 256
NORM_ROWS = 16
LEFT_COLS = 256
VMEM_BYTES = 40 * 2**20
WIDTH = 1
LOG2E = math.log2(math.e)
F32 = jnp.float32
BF16 = jnp.bfloat16
ALL = ("blk", "yl", "x", "core")


def norm_rows(points, norms_first):
    wide = points.astype(F32)
    norms = 5.0 * jnp.sum(wide * wide, axis=0, keepdims=True)
    high = norms.astype(BF16).astype(F32)
    middle = (norms - high).astype(BF16).astype(F32)
    low = norms - high - middle
    row = lax.broadcasted_iota(jnp.int32, (NORM_ROWS, norms.shape[1]), 0)
    at, ones_at = (0, 3) if norms_first else (3, 0)
    rows = jnp.where((row >= ones_at) & (row < ones_at + 3), 1.0, 0.0)
    for offset, part in enumerate((high, middle, low)):
        rows = jnp.where(row == at + offset, part, rows)
    return rows


def three_matern(five_dist_sq):
    clipped = jnp.maximum(five_dist_sq, 1e-30)
    spread = clipped * lax.rsqrt(clipped)
    return ((clipped + (3.0 * spread + 3.0)) * jnp.exp2(spread * (-LOG2E))).astype(BF16)


def left_rows(packet, feat):
    points = packet[:feat, :]
    wide = points.astype(F32)
    pad = jnp.zeros((LEFT_COLS - 2 * feat - NORM_ROWS, points.shape[1]), F32)
    whole = jnp.concatenate([wide * -8.0, wide * -2.0, norm_rows(points, True), pad], axis=0)
    return whole.T.astype(BF16)


def right_rows(right_ref, p, points):
    feat = points.shape[0]
    right_ref[p, :feat, :] = points
    right_ref[p, feat : 2 * feat, :] = points
    right_ref[p, 2 * feat :, :] = norm_rows(points, False).astype(BF16)


def add(sums, key, term):
    sums[key] = sums[key] + term if key in sums else term


def run_tiles(tiles, left_of, right_of, use):
    squares, values = {}, {}
    for t in range(len(tiles) + 2):
        if t < len(tiles):
            left, right = left_of(tiles[t]), right_of(tiles[t])
            squares[t] = jnp.dot(left, right, preferred_element_type=F32)
        if 1 <= t <= len(tiles):
            values[t - 1] = three_matern(squares.pop(t - 1))
        if t >= 2:
            use(tiles[t - 2], values.pop(t - 2))


def times_transposed(dirs, tile):
    return lax.dot_general(dirs, tile, (((1,), (1,)), ((), ())), preferred_element_type=F32)


def pair_kernel(feat, carry, *refs):
    refs = list(refs)
    fixed_refs = [refs.pop(0) for _ in range(ROUNDS)]
    moving_ref = refs.pop(0)
    carry_ref = refs.pop(0) if carry else None
    forward_ref, back_ref, left_ref, right_ref = refs
    rows = moving_ref.shape[2]
    depth = 2 * feat + NORM_ROWS

    @pl.when(pl.program_id(0) == 0)
    def _():
        for i, fixed_ref in enumerate(fixed_refs):
            left_ref[i] = left_rows(fixed_ref[...], feat)
        back_ref[...] = carry_ref[...] if carry else jnp.zeros_like(back_ref)

    right_rows(right_ref, 0, moving_ref[0, :feat, :])
    span = range(0, rows, SUB)
    tiles = [(i, c, r) for i in range(ROUNDS) for r in span for c in span]
    forward_sums, back_sums = {}, {}

    def use(place, tile):
        i, c, r = place
        dirs = fixed_refs[i][feat:, c : c + SUB]
        add(forward_sums, r, jnp.dot(dirs, tile, preferred_element_type=F32))
        add(back_sums, (i, c), times_transposed(moving_ref[0, feat:, r : r + SUB], tile))

    run_tiles(
        tiles,
        lambda place: left_ref[place[0], place[1] : place[1] + SUB, :depth],
        lambda place: right_ref[0, :, place[2] : place[2] + SUB],
        use,
    )
    for r, total in forward_sums.items():
        forward_ref[0, :, r : r + SUB] = (total * (1.0 / 3.0)).astype(forward_ref.dtype)
    for (i, c), total in back_sums.items():
        back_ref[i, :, c : c + SUB] += total * (1.0 / 3.0)


def cost(evals, products):
    return pl.CostEstimate(
        flops=2 * evals * 256 * products, bytes_accessed=evals // 16, transcendentals=2 * evals
    )


def pair_call(fixed, moving, feat, carry=None):
    count, height, rows = moving.shape
    cols = height - feat
    depth = 2 * feat + NORM_ROWS
    back_spec = pl.BlockSpec((ROUNDS, cols, rows), lambda j: (0, 0, 0))
    carried = [] if carry is None else [carry]
    return pl.pallas_call(
        functools.partial(pair_kernel, feat, bool(carried)),
        grid=(count,),
        in_specs=[pl.BlockSpec((height, rows), lambda j: (0, 0))] * ROUNDS
        + [pl.BlockSpec((1, height, rows), lambda j: (j, 0, 0))]
        + [back_spec] * len(carried),
        out_specs=[pl.BlockSpec((1, cols, rows), lambda j: (j, 0, 0)), back_spec],
        out_shape=[
            jax.ShapeDtypeStruct((count, cols, rows), BF16),
            jax.ShapeDtypeStruct((ROUNDS, cols, rows), F32),
        ],
        scratch_shapes=[
            pltpu.VMEM((ROUNDS, rows, LEFT_COLS), BF16),
            pltpu.VMEM((1, depth, rows), BF16),
        ],
        compiler_params=pltpu.CompilerParams(vmem_limit_bytes=VMEM_BYTES),
        cost_estimate=cost(ROUNDS * count * rows * rows, 3),
    )(*fixed, moving, *carried)


def own_kernel(feat, lanes, left_ref, *refs):
    refs = list(refs)
    lane_refs = [[refs.pop(0) for _ in counts] for counts in lanes]
    carry_ref, back_ref, right_ref, dirs_ref = refs
    rows = right_ref.shape[2]
    depth = 2 * feat + NORM_ROWS
    step = pl.program_id(0)

    @pl.when(step == 0)
    def _():
        back_ref[...] = carry_ref[...]

    for p, (counts, moving_refs) in enumerate(zip(lanes, lane_refs)):
        start = 0
        for count, moving_ref in zip(counts, moving_refs):

            @pl.when((step >= start) & (step < start + count))
            def _(p=p, moving_ref=moving_ref):
                right_rows(right_ref, p, moving_ref[0, :feat, :])
                dirs_ref[p] = moving_ref[0, feat:, :]

            start += count
    span = range(0, rows, SUB)
    back_sums = {}

    def use(place, tile):
        p, c, r = place
        add(back_sums, c, times_transposed(dirs_ref[p, :, r : r + SUB], tile))

    run_tiles(
        [(p, c, r) for p in range(len(lanes)) for c in span for r in span],
        lambda place: left_ref[place[1] : place[1] + SUB, :depth],
        lambda place: right_ref[place[0], :, place[2] : place[2] + SUB],
        use,
    )
    for c, total in back_sums.items():
        back_ref[:, c : c + SUB] += total * (1.0 / 3.0)


def own_call(left, lanes, carry, feat):
    _, height, rows = lanes[0][0][0].shape
    cols = height - feat
    counts = [[count for _, _, count in parts] for parts in lanes]
    steps = sum(counts[0])

    def block(start, first, count):
        return lambda j: (first + jnp.clip(j - start, 0, count - 1), 0, 0)

    moving_specs = [
        pl.BlockSpec((1, height, rows), block(sum(lane[:k]), first, count))
        for parts, lane in zip(lanes, counts)
        for k, (_, first, count) in enumerate(parts)
    ]
    return pl.pallas_call(
        functools.partial(own_kernel, feat, counts),
        grid=(steps,),
        in_specs=[pl.BlockSpec(left.shape, lambda j: (0, 0))]
        + moving_specs
        + [pl.BlockSpec((cols, rows), lambda j: (0, 0))],
        out_specs=pl.BlockSpec((cols, rows), lambda j: (0, 0)),
        out_shape=jax.ShapeDtypeStruct((cols, rows), F32),
        scratch_shapes=[
            pltpu.VMEM((len(lanes), 2 * feat + NORM_ROWS, rows), BF16),
            pltpu.VMEM((len(lanes), cols, rows), BF16),
        ],
        compiler_params=pltpu.CompilerParams(vmem_limit_bytes=VMEM_BYTES),
        cost_estimate=cost(len(lanes) * steps * rows * rows, 2),
    )(left, *[moving for parts in lanes for moving, _, _ in parts], carry)


def short_kernel(feat, first, count, width, left_ref, moving_ref, carry_ref, back_ref, right_ref):
    rows = moving_ref.shape[2]
    depth = 2 * feat + NORM_ROWS
    steps = rows // (width * SUB)
    back_ref[...] = carry_ref[...]

    def prepare(p, _):
        right_rows(right_ref, p, moving_ref[first + p, :feat, :])
        return 0

    lax.fori_loop(0, count, prepare, 0)

    def step(at, _):
        p, start = at // steps, (at % steps) * (width * SUB)
        back_sums = {}

        def use(place, tile):
            c, r = place
            add(back_sums, c, times_transposed(moving_ref[first + p, feat:, r : r + SUB], tile))

        run_tiles(
            [(c * SUB, r) for c in range(width) for r in range(0, rows, SUB)],
            lambda place: left_ref[pl.ds(pl.multiple_of(start + place[0], SUB), SUB), :depth],
            lambda place: right_ref[p, :, place[1] : place[1] + SUB],
            use,
        )
        for c, total in back_sums.items():
            span = pl.ds(pl.multiple_of(start + c, SUB), SUB)
            back_ref[:, span] += total * (1.0 / 3.0)
        return 0

    lax.fori_loop(0, count * steps, step, 0)


def short_call(left, moving, carry, feat, first, count, width=WIDTH):
    _, height, rows = moving.shape
    return pl.pallas_call(
        functools.partial(short_kernel, feat, first, count, width),
        out_shape=jax.ShapeDtypeStruct((height - feat, rows), F32),
        scratch_shapes=[pltpu.VMEM((count, 2 * feat + NORM_ROWS, rows), BF16)],
        compiler_params=pltpu.CompilerParams(vmem_limit_bytes=VMEM_BYTES),
        cost_estimate=cost(count * rows * rows, 2),
    )(left, moving, carry)


def left_call(packet, feat):
    def kernel(packet_ref, left_ref):
        left_ref[...] = left_rows(packet_ref[...], feat)

    return pl.pallas_call(
        kernel, out_shape=jax.ShapeDtypeStruct((packet.shape[1], LEFT_COLS), BF16)
    )(packet)


def pair_routes(mask, blocks, cores):
    routes = []
    for block in range(blocks):
        other = block ^ mask
        for core in range(cores):
            from_core = core if block < other else core ^ 1
            routes.append((other * cores + from_core, block * cores + core))
    return routes


def over_pair(mask, array, work, *operands):
    blocks, cores = lax.axis_size("blk"), lax.axis_size("core")

    def branch(known):
        def send(value, *operands):
            routes = pair_routes(known, blocks, cores)
            return lax.ppermute(value, ("blk", "core"), routes), work(*operands)

        return send

    return lax.switch(mask - 1, [branch(known) for known in range(1, blocks)], array, *operands)


def swap(array, axis, distance=1):
    return lax.ppermute(array, axis, [(i, i ^ distance) for i in range(lax.axis_size(axis))])


def shards(features, inv_scale, direction, residual, noise_variance, plan):
    feat = features.shape[1]
    rows, cols = direction.shape
    x_size = lax.axis_size("x")
    scaled = (features.astype(F32) * inv_scale).astype(BF16)
    packet = jnp.concatenate([scaled.T, direction.T], axis=0)

    def short(first, count):
        return lambda left, moving, carry: short_call(left, moving, carry, feat, first, count)

    def own_tiles(own, *lanes):
        return own_call(left, lanes, own, feat)

    left = left_call(packet, feat)
    near = [packet] + [swap(packet, "x", shift) for shift in range(1, x_size)]
    own = jnp.zeros((cols, rows), F32)
    first_partner, own = over_pair(plan[0], packet, short(0, 1), left, packet[None], own)
    near = jnp.stack(near)
    second_partner, own = over_pair(plan[1], packet, short(1, 2), left, near, own)
    near, second_partner = lax.optimization_barrier((near, second_partner))
    partners = [first_partner, second_partner]
    far = swap(near, "yl")
    near_mates = swap(near, "core")
    near_forward, back = pair_call(partners, near, feat)
    own = own_tiles(own, [(near, 3, 1), (near_mates, 0, 2)])
    far, own = lax.optimization_barrier((far, own))
    far_mates = swap(far, "core")
    far_forward, back = pair_call(partners, far, feat, back)

    masks = plan[:ROUNDS]
    position = lax.axis_index("blk")
    follower = position > jnp.bitwise_xor(position, masks)

    def taken(at):
        return jnp.bitwise_and(jnp.right_shift(masks, at), 1)[:, None, None] == 1

    sums = jnp.stack([near_forward, far_forward])
    back = back.astype(BF16)
    arrived = swap(back, "core")
    shares = [swap(sums[:, shift], "x", shift) for shift in range(1, x_size)]
    own = own_tiles(own, [(near_mates, 2, x_size - 2), (far, 0, 1)])
    arrived, own = lax.optimization_barrier((arrived, own))
    back = jnp.where(follower[:, None, None], arrived, back)

    arrived = swap(back, "blk", 1)
    own = own_tiles(own, [(far, 1, x_size - 1)])
    arrived, shares, own = lax.optimization_barrier((arrived, shares, own))
    back = jnp.where(taken(0), arrived, back)
    halves = sums[:, 0].astype(F32)
    for share in shares:
        halves = halves + share.astype(F32)

    arrived = [swap(back, "blk", distance) for distance in (2, 4, 6)]
    share = swap(halves[1].astype(BF16), "yl")
    own = own_tiles(own, [(far_mates, 0, 2)], [(far_mates, 2, 2)])
    (one, two, both), share, own = lax.optimization_barrier((arrived, share, own))
    total = halves[0] + share.astype(F32)
    back = jnp.where(taken(2), jnp.where(taken(1), both, two), jnp.where(taken(1), one, back))
    wide_dirs = direction.T.astype(F32)
    product = own + total + jnp.sum(back.astype(F32), axis=0)
    product = product + noise_variance[0] * wide_dirs
    inner = jnp.stack([jnp.sum(wide_dirs * product, axis=1), jnp.sum(residual.T * product, axis=1)])
    device_count = math.prod(lax.axis_size(axis) for axis in ALL)
    copies = jnp.broadcast_to(inner.reshape(1, 2 * cols), (device_count, 2 * cols))
    partials = lax.all_to_all(copies, ALL, 0, 0, tiled=True)
    totals = jnp.sum(partials, axis=0).reshape(2, cols)
    return (product.T, totals / (rows * device_count))


def solution(mesh):
    yl_size, cores = 2, 2
    groups = mesh.shape["sub"]
    split = mesh.devices.reshape(mesh.shape["blk"], yl_size, groups // (yl_size * cores), cores)
    by_rows = P(ALL, None)
    return jax.shard_map(
        shards,
        mesh=Mesh(split, ALL),
        in_specs=(by_rows, P(), by_rows, by_rows, P(), P()),
        out_specs=(by_rows, P()),
        check_vma=False,
    )
```
